128 devices in a mesh: grp: 16 (over y, z_lo, core), sub: 8 (over x, z_hi).
Axes of the slice: x: 4, y: 4, z: 4 (z_hi: 2, z_lo: 2; z = z_hi * 2 + z_lo), core: 2. Of those that a mesh axis runs over, the one named last changes fastest.
Arguments:
- node_feats: bfloat16 [262144, 512], P(('grp', 'sub')), may hold values from -6 to 6
- node_grad: bfloat16 [262144, 512], P(('grp', 'sub')), may hold values from -6 to 6
- small_edges: bfloat16 [32768, 512], P(('grp', 'sub')), may hold values from -6 to 6
- giant_edges: bfloat16 [2048, 512], P(('grp', 'sub')), may hold values from -6 to 6
- pair_node: int32 [131072], P(('grp', 'sub')), may hold values from 0 to 262143, as said below
- pair_edge: int32 [131072], P(('grp', 'sub')), may hold values from 0 to 383
- send_count: int32 [128, 128], P(('grp', 'sub')), may hold values from 2 to 8, as said below
- w_in: bfloat16 [1024, 512], replicated, may hold values from -0.1875 to 0.1875
- b_in: float32 [512], replicated, may hold values from -4 to 4
- w_out: bfloat16 [512, 512], replicated, may hold values from -0.25 to 0.25
Outputs:
- grad_nodes: bfloat16 [262144, 512], P(('grp', 'sub'))
- grad_small: bfloat16 [32768, 512], P(('grp', 'sub'))
- grad_giant: bfloat16 [2048, 512], P(('grp', 'sub'))
- grad_w_in: float32 [1024, 512], replicated
- grad_b_in: float32 [512], replicated
- grad_w_out: float32 [512, 512], replicated
The draws below stay inside these ranges and needn't reach their ends.
Inputs may be any that keep to these rules, and one draw needn't show every extreme that they name: `pair_node`: slots of bucket j on any device hold nodes owned by device j, ids j * 2048 to (j + 1) * 2048 - 1. `send_count`: no entry exceeds 8; in every draw some owner gets 8 live slots from every device.
All inputs are finite; a program needn't handle non-finite values.
Results may differ from the reference program's by a relative error of at most 0.017.
Values may be sent and summed in bfloat16 or wider, within the bound.
A program may use at most 128 MiB of HBM per device.

```python
import jax
import jax.numpy as jnp
from jax import lax

C = 512
H = 512
PAIR_DEV = 1024
NODE_DEV = 2048
E_SMALL = 256
GIANT_DEV = 16
CAP = 8
PAIRS = 131072
NODES = 262144
SMALL_ALL = 32768
GIANT_ALL = 2048
N_SUB = 8
DEVICES = 128


def draw_pair_node(key, part):
    key = jax.random.fold_in(key, 11)
    positions = jnp.arange(PAIRS, dtype=jnp.int32)
    bucket = positions % PAIR_DEV // CAP
    offsets = jax.random.randint(key, (PAIRS,), 0, NODE_DEV, dtype=jnp.int32)
    return bucket * NODE_DEV + offsets


def draw_send_count(key, part):
    key = jax.random.fold_in(key, 23)
    key_base, key_owner = jax.random.split(key)
    lowest = max(1, CAP // 4)
    base_count = jax.random.randint(key_base, (DEVICES, DEVICES), lowest, CAP + 1, dtype=jnp.int32)
    hot_owner = jax.random.randint(key_owner, (), 0, DEVICES, dtype=jnp.int32)
    column = jnp.arange(DEVICES, dtype=jnp.int32)[None, :]
    return jnp.where(column == hot_owner, CAP, base_count).astype(jnp.int32)


def touch_ends(array, rng, smallest, high):
    extent = array.shape
    place = [jax.random.randint(jax.random.fold_in(rng, axis), (), 0, extent[axis]) for axis in range(len(extent))]
    array = array.at[tuple(place)].set(smallest)
    longest = extent.index(max(extent))
    place[longest] = (place[longest] + 1) % extent[longest]
    return array.at[tuple(place)].set(high)


def block_levels(stream_key, extent, cuts, low, largest):
    loudness = 1.0
    for axis_at, parts in cuts:
        steps = jax.random.uniform(jax.random.fold_in(jax.random.fold_in(stream_key, 6), axis_at), (parts,), jnp.float32, low / len(cuts), largest / len(cuts))
        loudness = loudness * jnp.repeat(jnp.exp(steps), extent[axis_at] // parts).reshape((-1,) + (1,) * (len(extent) - 1 - axis_at))
    return loudness


def scatter_about(own_key, shape, spread, limit, cuts=(), held_as=jnp.bfloat16):
    values = spread * jax.random.normal(own_key, shape, jnp.float32)
    if cuts:
        values = values * block_levels(own_key, shape, cuts, -0.22, 0.18)
    return jnp.clip(values, -limit, limit).astype(held_as)


def setup_inputs(seed: int = 0) -> dict:
    seeds = jax.random.split(jax.random.key(seed), 11)
    node_feats = scatter_about(seeds[0], (NODES, C), 1.0, 6.0, ((0, 128),))
    node_grad = scatter_about(seeds[1], (NODES, C), 1.0, 6.0, ((0, 128),))
    small_edges = scatter_about(seeds[2], (SMALL_ALL, C), 1.0, 6.0, ((0, 128),))
    giant_edges = scatter_about(seeds[3], (GIANT_ALL, C), 1.0, 6.0, ((0, 128),))
    pair_node = draw_pair_node(jax.random.fold_in(seeds[10], 71), 0)
    pair_edge = touch_ends(jax.random.randint(seeds[5], (PAIRS,), 0, E_SMALL + GIANT_DEV * N_SUB), jax.random.fold_in(seeds[5], 1), 0, (E_SMALL + GIANT_DEV * N_SUB) - 1).astype(jnp.int32)
    send_count = draw_send_count(jax.random.fold_in(seeds[10], 71), 0)
    w_in = scatter_about(seeds[7], (2 * C, H), (2 * C) ** -0.5, 0.1875)
    b_in = scatter_about(seeds[8], (H,), 1.0, 4.0, (), jnp.float32)
    w_out = scatter_about(seeds[9], (H, C), H ** -0.5, 0.25)
    return dict(node_feats=node_feats, node_grad=node_grad, small_edges=small_edges, giant_edges=giant_edges, pair_node=pair_node, pair_edge=pair_edge, send_count=send_count, w_in=w_in, b_in=b_in, w_out=w_out)


def reference(node_feats, node_grad, small_edges, giant_edges, pair_node, pair_edge, send_count, w_in, b_in, w_out):
    group_rows = GIANT_DEV * N_SUB

    def block_terms(carry, device):
        node_total, giant_total, grad_in, grad_bias, grad_out = carry
        group = device // N_SUB
        node_ids = lax.dynamic_slice_in_dim(pair_node, device * PAIR_DEV, PAIR_DEV)
        edge_ids = lax.dynamic_slice_in_dim(pair_edge, device * PAIR_DEV, PAIR_DEV)
        positions = jnp.arange(PAIR_DEV, dtype=jnp.int32)
        counts = lax.dynamic_index_in_dim(send_count, device, 0, keepdims=False)
        live_slot = (positions % CAP) < counts[positions // CAP]
        small_rows = lax.dynamic_slice_in_dim(small_edges, (device * E_SMALL).astype(jnp.int32), E_SMALL)
        giant_start = (group * group_rows).astype(jnp.int32)
        giant_block = lax.dynamic_slice_in_dim(giant_edges, giant_start, group_rows)
        edge_table = jnp.concatenate([small_rows, giant_block], axis=0)
        joined = jnp.concatenate([jnp.take(node_feats, node_ids, axis=0), jnp.take(edge_table, edge_ids, axis=0)], axis=1)
        preact = jnp.dot(joined, w_in, preferred_element_type=jnp.float32) + b_in
        logistic = jax.nn.sigmoid(preact)
        hidden = (preact * logistic).astype(jnp.bfloat16)
        out_grad = jnp.where(live_slot[:, None], jnp.take(node_grad, node_ids, axis=0), jnp.zeros((), jnp.bfloat16)).astype(jnp.bfloat16)
        grad_out = grad_out + jnp.dot(hidden.T, out_grad, preferred_element_type=jnp.float32)
        hid_grad = jnp.dot(out_grad, w_out.T, preferred_element_type=jnp.float32)
        pre_grad = (hid_grad * logistic * (1.0 + preact * (1.0 - logistic))).astype(jnp.bfloat16)
        grad_in = grad_in + jnp.dot(joined.T, pre_grad, preferred_element_type=jnp.float32)
        grad_bias = grad_bias + jnp.sum(pre_grad.astype(jnp.float32), axis=0)
        in_grad = jnp.dot(pre_grad, w_in.T, preferred_element_type=jnp.float32)
        node_term = in_grad[:, :C].astype(jnp.bfloat16).astype(jnp.float32)
        edge_term = in_grad[:, C:]
        node_total = node_total.at[node_ids].add(node_term)
        edge_sum = jax.ops.segment_sum(edge_term, edge_ids, num_segments=E_SMALL + group_rows)
        old_giant = lax.dynamic_slice_in_dim(giant_total, giant_start, group_rows)
        giant_total = lax.dynamic_update_slice_in_dim(giant_total, old_giant + edge_sum[E_SMALL:], giant_start, 0)
        return (node_total, giant_total, grad_in, grad_bias, grad_out), edge_sum[:E_SMALL].astype(jnp.bfloat16)

    start_carry = (jnp.zeros((NODES, C), jnp.float32), jnp.zeros((GIANT_ALL, C), jnp.float32),
                   jnp.zeros((2 * C, H), jnp.float32), jnp.zeros((H,), jnp.float32), jnp.zeros((H, C), jnp.float32))
    final, small_blocks = lax.scan(block_terms, start_carry, jnp.arange(DEVICES, dtype=jnp.int32))
    node_total, giant_total, grad_in, grad_bias, grad_out = final
    grad_nodes = (node_grad.astype(jnp.float32) + node_total).astype(jnp.bfloat16)
    grad_small = small_blocks.reshape(SMALL_ALL, C)
    return grad_nodes, grad_small, giant_total.astype(jnp.bfloat16), grad_in, grad_bias, grad_out
```

```python
import functools

import jax
import jax.numpy as jnp
from jax import lax
from jax.experimental import pallas as pl
from jax.experimental.pallas import tpu as pltpu
from jax.sharding import PartitionSpec as P

MESH = pl.DeviceIdType.MESH


def mask_of(s):
    core, par, y, x, zh = (s >> 6) & 1, (s >> 5) & 1, (s >> 3) & 3, (s >> 1) & 3, s & 1
    zl = par ^ (x & 1) ^ (y & 1)
    return (y << 5) | (zl << 4) | (core << 3) | (x << 1) | zh


def place(j):
    return (j // 8, lax.rem(j, 8))


def exchange_kernel(count, x_ref, o_ref, send_sem, recv_sem):
    me = lax.axis_index("grp") * 8 + lax.axis_index("sub")
    barrier = pltpu.get_barrier_semaphore()

    def greet(s, carry):
        pl.semaphore_signal(barrier, inc=1, device_id=place(me ^ s), device_id_type=MESH)
        return carry

    lax.fori_loop(1, count, greet, 0)
    pl.semaphore_wait(barrier, count - 1)

    def send(s, carry):
        j = me ^ mask_of(s)
        pltpu.make_async_remote_copy(
            src_ref=x_ref.at[j],
            dst_ref=o_ref.at[me],
            send_sem=send_sem,
            recv_sem=recv_sem,
            device_id=place(j),
            device_id_type=MESH,
        ).start()
        return carry

    lax.fori_loop(1, count, send, 0)
    o_ref[me] = x_ref[me]
    whole = pltpu.make_async_remote_copy(
        src_ref=x_ref.at[pl.ds(1, count - 1)],
        dst_ref=o_ref.at[pl.ds(1, count - 1)],
        send_sem=send_sem,
        recv_sem=recv_sem,
        device_id=place(me ^ 1),
        device_id_type=MESH,
    )
    whole.wait_recv()
    whole.wait_send()


def exchange(values, number):
    count = values.shape[0]
    return pl.pallas_call(
        functools.partial(exchange_kernel, count),
        out_shape=jax.ShapeDtypeStruct(values.shape, values.dtype),
        in_specs=[pl.BlockSpec(memory_space=pltpu.VMEM)],
        out_specs=pl.BlockSpec(memory_space=pltpu.VMEM),
        scratch_shapes=[pltpu.SemaphoreType.DMA, pltpu.SemaphoreType.DMA],
        compiler_params=pltpu.CompilerParams(
            collective_id=number, has_side_effects=True, vmem_limit_bytes=32 << 20
        ),
    )(values)


def shards(
    node_feats,
    node_grad,
    small_edges,
    giant_edges,
    pair_node,
    pair_edge,
    send_count,
    w_in,
    b_in,
    w_out,
):
    grp_count = lax.axis_size("grp")
    sub_count = lax.axis_size("sub")
    devices = grp_count * sub_count
    pair_count = pair_node.shape[0]
    capacity = pair_count // devices
    node_dev = node_feats.shape[0]
    feat_width = node_feats.shape[1]
    small_count = small_edges.shape[0]
    giant_dev = giant_edges.shape[0]
    local_index = (pair_node % node_dev).reshape(devices, capacity)
    requested = exchange(jnp.pad(local_index, ((0, 0), (0, 120))).reshape(devices, 1, 128), 1)[:, 0, :8].reshape(pair_count)
    owner_table = jnp.concatenate([node_feats, node_grad], axis=1)
    served = jnp.take(owner_table, requested, axis=0).reshape(devices, capacity, 2 * feat_width)
    fetched = exchange(served, 2).reshape(pair_count, 2 * feat_width)
    positions = jnp.arange(pair_count, dtype=jnp.int32)
    live_slot = positions % capacity < send_count[0][positions // capacity]
    giant_group = lax.all_gather(giant_edges, "sub", axis=0, tiled=True)
    edge_table = jnp.concatenate([small_edges, giant_group], axis=0)
    joined = jnp.concatenate(
        [fetched[:, :feat_width], jnp.take(edge_table, pair_edge, axis=0)], axis=1
    )
    preact = jnp.dot(joined, w_in, preferred_element_type=jnp.float32) + b_in
    logistic = jax.nn.sigmoid(preact)
    hidden = (preact * logistic).astype(jnp.bfloat16)
    out_grad = jnp.where(live_slot[:, None], fetched[:, feat_width:], jnp.zeros((), jnp.bfloat16))
    grad_out = jnp.einsum("ph,pc->hc", hidden, out_grad, preferred_element_type=jnp.float32)
    hid_grad = jnp.einsum("pc,hc->ph", out_grad, w_out, preferred_element_type=jnp.float32)
    pre_grad = (hid_grad * logistic * (1.0 + preact * (1.0 - logistic))).astype(jnp.bfloat16)
    grad_in = jnp.einsum("pk,ph->kh", joined, pre_grad, preferred_element_type=jnp.float32)
    grad_bias = jnp.sum(pre_grad.astype(jnp.float32), axis=0)
    in_grad = jnp.einsum("ph,kh->pk", pre_grad, w_in, preferred_element_type=jnp.float32)
    node_term = in_grad[:, :feat_width].astype(jnp.bfloat16).reshape(devices, capacity, feat_width)
    edge_term = in_grad[:, feat_width:]
    returned = exchange(node_term, 3).reshape(pair_count, feat_width)
    node_sum = jax.ops.segment_sum(returned.astype(jnp.float32), requested, num_segments=node_dev)
    grad_nodes = (node_grad.astype(jnp.float32) + node_sum).astype(jnp.bfloat16)
    edge_sum = jax.ops.segment_sum(
        edge_term, pair_edge, num_segments=small_count + giant_group.shape[0]
    )
    grad_small = edge_sum[:small_count].astype(jnp.bfloat16)
    giant_part = edge_sum[small_count:]
    giant_total = lax.psum(giant_part.astype(jnp.bfloat16), "sub").astype(jnp.float32)
    giant_mine = lax.dynamic_slice_in_dim(
        giant_total, lax.axis_index("sub") * giant_dev, giant_dev, 0
    )
    grad_in, grad_bias, grad_out = lax.psum((grad_in, grad_bias, grad_out), ("grp", "sub"))
    return (grad_nodes, grad_small, giant_mine.astype(jnp.bfloat16), grad_in, grad_bias, grad_out)


def solution(mesh):
    placed = (
        P(("grp", "sub"), None),
        P(("grp", "sub"), None),
        P(("grp", "sub"), None),
        P(("grp", "sub"), None),
        P(("grp", "sub")),
        P(("grp", "sub")),
        P(("grp", "sub"), None),
        P(),
        P(),
        P(),
    )
    return jax.shard_map(
        shards,
        mesh=mesh,
        in_specs=placed,
        out_specs=(
            P(("grp", "sub"), None),
            P(("grp", "sub"), None),
            P(("grp", "sub"), None),
            P(),
            P(),
            P(),
        ),
        check_vma=False,
    )
```

```python
import functools

import jax
import jax.numpy as jnp
from jax import lax
from jax.experimental import pallas as pl
from jax.experimental.pallas import tpu as pltpu
from jax.sharding import PartitionSpec as P

MESH = pl.DeviceIdType.MESH
BF = jnp.bfloat16
F32 = jnp.float32
I32 = jnp.int32
DEVICES = 128
SUB = 8
GRP = 16
CAP = 8
SLOTS = 1024
WIDTH = 512
NODES = 2048
SMALL = 256
GIANT = 16
EDGES = SMALL + GIANT * SUB
CHUNKS = 4
PER = DEVICES // CHUNKS
ROWS = PER * CAP


def device_of(x, y, z, core):
    return (y * 4 + (z & 1) * 2 + core, x * 2 + (z >> 1))


def mask_of(s):
    core, par, y, x, zh = (s >> 6) & 1, (s >> 5) & 1, (s >> 3) & 3, (s >> 1) & 3, s & 1
    zl = par ^ (x & 1) ^ (y & 1)
    return (y << 5) | (zl << 4) | (core << 3) | (x << 1) | zh


def place(j):
    return (j // SUB, lax.rem(j, SUB))


def dot(a, b, ca=1, cb=0):
    return lax.dot_general(
        a, b, (((ca,), (cb,)), ((), ())), preferred_element_type=F32
    )


def remote(src, dst, send, recv, to):
    return pltpu.make_async_remote_copy(
        src_ref=src, dst_ref=dst, send_sem=send, recv_sem=recv, device_id=to, device_id_type=MESH
    )


def loop(low, high, step):
    def body(i, carry):
        step(i)
        return carry

    lax.fori_loop(low, high, body, 0)


def layer_kernel(
    nf_in, ng_in, small_in, giant_in, pn_in, pe_in, sc_in, win_in, bin_in, wout_in,
    nodes_out, small_out, giant_out, w_out, bias_out,
    nf, ng, win, wout, b_in, pn, pe, sc,
    etab, one_t, ix1, ixt, ix2, colb, rowb,
    esend, erecv, tsend, trecv, nd_all, og_all, pg_all, nt, nodes, smalls, giants,
    gw, gb, S, r0, S1, r1, S2, r2, G, bb0, bb1, bb2, bfin, gsend, grecv,
    in_sem, out_sem, gi_s, gi_r, i1_s, i1_r, i2_s, i2_r, e_s, e_r, t_s, t_r,
    w_s, w_r, b_s, b_r, gg_s, gg_r,
):
    g, u = lax.axis_index("grp"), lax.axis_index("sub")
    me = g * SUB + u
    y, zl, core, x, zh = g >> 2, (g >> 1) & 1, g & 1, u >> 1, u & 1
    z = zh * 2 + zl
    par = zl ^ (x & 1) ^ (y & 1)
    pm = (core << 6) | (par << 5) | (y << 3) | (x << 1) | zh
    there = (x, y, z)
    axis1 = (x, y, z)
    index2 = (y * 4 + z, z * 4 + x, x * 4 + y)

    def peer1(p, k):
        c = list(there)
        c[p] = k
        return device_of(c[0], c[1], c[2], core)

    def peer2(p, k):
        c = list(there)
        c[(p + 1) % 3] = k >> 2
        c[(p + 2) % 3] = k & 3
        return device_of(c[0], c[1], c[2], core)

    mine = pl.ds(pl.multiple_of(SMALL + u * GIANT, GIANT), GIANT)
    loads = [
        pltpu.make_async_copy(a, b, in_sem.at[i])
        for i, (a, b) in enumerate(
            (
                (pn_in, pn), (sc_in, sc), (giant_in, etab.at[mine]), (pe_in, pe),
                (small_in, etab.at[pl.ds(0, SMALL)]), (nf_in, nf), (ng_in, ng),
                (win_in, win), (wout_in, wout), (bin_in, b_in),
            )
        )
    ]
    for load in loads:
        load.start()

    barrier = pltpu.get_barrier_semaphore()
    loop(1, SUB, lambda o: pl.semaphore_signal(
        barrier, inc=1, device_id=(g, u ^ o), device_id_type=MESH))
    loop(1, GRP, lambda o: pl.semaphore_signal(
        barrier, inc=1, device_id=(g ^ o, u), device_id_type=MESH))

    loads[0].wait()
    loads[1].wait()
    r_at = lax.broadcasted_iota(I32, (8, 128), 0)
    l_at = lax.broadcasted_iota(I32, (8, 128), 1)
    spread = jnp.where((l_at >> 4) == r_at, sc[...].astype(F32), 0.0).astype(BF)
    j_at = lax.broadcasted_iota(I32, (128, 128), 0)
    p_at = lax.broadcasted_iota(I32, (128, 128), 1)
    expand = jnp.where((j_at & 15) == (p_at >> 3), 1.0, 0.0).astype(BF)
    counts = dot(spread, expand).astype(I32)
    packed = jnp.where((l_at & 7) < counts, pn[...] & (NODES - 1), 4095)
    ix1[u] = packed
    loads[2].wait()

    bb0[core] = jnp.zeros((8, 128), F32)

    pl.semaphore_wait(barrier, SUB + GRP - 2)

    def step1(o):
        to = (g, u ^ o)
        remote(ix1.at[u], ix1.at[u], i1_s, i1_r, to).start()
        remote(etab.at[mine], etab.at[mine], gi_s, gi_r, to).start()

    loop(1, SUB, step1)
    loads[3].wait()
    one_t[...] = jnp.where(
        lax.broadcasted_iota(I32, (EDGES, SLOTS), 0) == pe[...], 1.0, 0.0
    ).astype(BF)
    loads[4].wait()

    others = remote(ix1.at[pl.ds(0, SUB - 1)], ix1.at[pl.ds(0, SUB - 1)], i1_s, i1_r, (g, u ^ 1))
    others.wait_recv()

    for r in range(8):
        ixt[r] = jnp.concatenate([ix1[k, r : r + 1, :] for k in range(SUB)], axis=0)

    def step2(o):
        h = g ^ o
        remote(ixt.at[h >> 1], ix2.at[g], i2_s, i2_r, (h, u)).start()

    loop(1, GRP, step2)
    ix2[g] = ixt[g >> 1]

    span = pl.ds(SMALL, (SUB - 1) * GIANT)
    rows_in = remote(etab.at[span], etab.at[span], gi_s, gi_r, (g, u ^ 1))
    rows_in.wait_recv()
    esend[...] = dot(one_t[...], etab[...], 0, 0).astype(BF).reshape(DEVICES, CAP, WIDTH)

    def send_rows(s):
        j = me ^ mask_of(s)
        remote(esend.at[j], erecv.at[pm], e_s, e_r.at[s >> 5], place(j)).start()

    loop(1, DEVICES, send_rows)
    erecv[pm] = esend[me]

    half = ix2.at[pl.ds(0, GRP - 1)]
    terms_in = remote(half, half, i2_s, i2_r, (g ^ 1, u))
    terms_in.wait_recv()
    table = ix2[...].reshape(DEVICES, 128)
    high, low = (table >> 8).astype(F32).astype(BF), (table & 255).astype(F32).astype(BF)

    def source(q):
        qy, qx = (q >> 3) & 3, (q >> 1) & 3
        qz = ((q >> 5) & 1) ^ (qx & 1) ^ (qy & 1)
        return (qy << 5) | (qz << 4) | (((q >> 6) & 1) << 3) | (qx << 1) | (q & 1)

    first = (me & 15) * CAP
    s_col = lax.broadcasted_iota(I32, (SLOTS, 128), 0)
    d_col = lax.broadcasted_iota(I32, (SLOTS, 128), 1)
    pick = jnp.where(source(s_col >> 3) == d_col, 1.0, 0.0).astype(BF)
    values = dot(pick, high) * 256.0 + dot(pick, low)
    values = jnp.where(d_col == first + (s_col & 7), values, 0.0)
    col = jnp.sum(values, axis=1, keepdims=True).astype(I32)
    colb[...] = jnp.broadcast_to(col, (SLOTS, 128))
    values = dot(high, pick, 0, 1) * 256.0 + dot(low, pick, 0, 1)
    l_row = lax.broadcasted_iota(I32, (128, SLOTS), 0)
    s_row = lax.broadcasted_iota(I32, (128, SLOTS), 1)
    values = jnp.where(l_row == first + (s_row & 7), values, 0.0)
    rowb[...] = jnp.sum(values, axis=0, keepdims=True).astype(I32)

    for load in loads[5:]:
        load.wait()
    gw[...] = jnp.zeros_like(gw)
    gb[...] = jnp.zeros_like(gb)

    def chunk(c, last=False):
        b = (pm >> 5) ^ c
        rows = pl.ds(pl.multiple_of(b * ROWS, ROWS), ROWS)
        blocks = pl.ds(pl.multiple_of(b * PER, PER), PER)
        at = colb[rows]
        lanes = lax.broadcasted_iota(I32, (ROWS, 128), 1)
        hot = jnp.concatenate(
            [jnp.where(at == lanes + k * 128, 1.0, 0.0).astype(BF) for k in range(NODES // 128)],
            axis=1,
        )
        nd = dot(hot, nf[...]).astype(BF)
        og = dot(hot, ng[...]).astype(BF)
        nd_all[rows] = nd
        og_all[rows] = og
        preact = dot(nd, win[pl.ds(0, WIDTH)]) + b_in[...]
        hid_grad = dot(og, wout[...], 1, 1)

        if last:
            w = erecv.at[pl.ds(0, PER)]
            remote(w, w, e_s, e_r.at[c], (g, u ^ 1)).wait_recv()
        else:

            @pl.when(c == 0)
            def _():
                w = erecv.at[pl.ds(0, PER - 1)]
                remote(w, w, e_s, e_r.at[0], (g, u ^ 1)).wait_recv()

            @pl.when(c > 0)
            def _():
                w = erecv.at[pl.ds(0, PER)]
                remote(w, w, e_s, e_r.at[c], (g, u ^ 1)).wait_recv()

        er = erecv[blocks].reshape(ROWS, WIDTH)
        preact = preact + dot(er, win[pl.ds(WIDTH, WIDTH)])
        logistic = jax.nn.sigmoid(preact)
        hidden = (preact * logistic).astype(BF)
        pg = (hid_grad * logistic * (1.0 + preact * (1.0 - logistic))).astype(BF)
        pg_all[rows] = pg

        def weights(k, left, right):
            gw[pl.ds(k * WIDTH, WIDTH)] += dot(left, right, 0, 0)
            if last:
                reduce0(k)

        def terms():
            term = dot(pg, win[pl.ds(WIDTH, WIDTH)], 1, 1).astype(BF)
            tsend[blocks] = term.reshape(PER, CAP, WIDTH)

        if not last:
            terms()
            send_terms(c)
        weights(0, nd, pg)
        weights(1, er, pg)
        weights(2, hidden, og)
        gb[...] += jnp.sum(pg.astype(F32), axis=0, keepdims=True)
        if last:
            terms()

    def send_terms(c):
        def one(s):
            j = me ^ mask_of(s)
            remote(tsend.at[pm ^ s], trecv.at[me], t_s, t_r, place(j)).start()

        loop(c * PER + jnp.where(c == 0, 1, 0), (c + 1) * PER, one)

    twin = (g ^ 1, u)

    def reduce0(p):
        for h in range(2):
            for i in range(4):
                top, left = WIDTH * p + 256 * (i >> 1), 256 * h + 128 * (i & 1)
                S[h, p, i] = gw[top : top + 256, left : left + 128].astype(BF)
        remote(S.at[1 - core, p], r0.at[p], w_s.at[0, p], w_r.at[0, p], twin).start()

    loop(0, CHUNKS - 1, chunk)
    chunk(CHUNKS - 1, True)
    trecv[me] = tsend[pm]
    for i in range(4):
        bb0[core, i : i + 1, :] = gb[:, 128 * i : 128 * i + 128]
    bias0 = remote(bb0.at[core], bb0.at[core], b_s.at[0], b_r.at[0], twin)
    bias0.start()

    nt[...] = dot(pg_all[...], win[pl.ds(0, WIDTH)], 1, 1).astype(BF)

    def node_tile(t):
        rows = pl.ds(pl.multiple_of(t * 256, 256), 256)
        hot = jnp.where(
            lax.broadcasted_iota(I32, (256, SLOTS), 0) + t * 256 == rowb[...], 1.0, 0.0
        ).astype(BF)
        nodes[rows] = (ng[rows].astype(F32) + dot(hot, nt[...])).astype(BF)

    def settle(ref, stage, p):
        done = remote(ref, ref, w_s.at[stage, p], w_r.at[stage, p], twin)
        done.wait_recv()
        waits.append(done)

    waits = [bias0]
    loop(0, 2, node_tile)
    for p in range(3):
        settle(r0.at[p], 0, p)
        for i in range(4):
            rows, half = pl.ds(WIDTH * p + 256 * (i >> 1), 256), pl.ds(pl.multiple_of(256 * core + 128 * (i & 1), 128), 128)
            S1[p, i] = (gw[rows, half] + r0[p, i].astype(F32)).astype(BF)
        for o in range(1, 4):
            k = axis1[p] ^ o
            remote(S1.at[p, k], r1.at[p, axis1[p]], w_s.at[1, p], w_r.at[1, p], peer1(p, k)).start()
        r1[p, axis1[p]] = S1[p, axis1[p]]
    bias0.wait_recv()
    bb1[x] = bb0[0] + bb0[1]
    for o in range(1, 4):
        remote(bb1.at[x], bb1.at[x], b_s.at[1], b_r.at[1], peer1(0, x ^ o)).start()
    send_terms(CHUNKS - 1)

    loop(2, NODES // 256, node_tile)
    put_nodes = pltpu.make_async_copy(nodes, nodes_out, out_sem.at[0])
    put_nodes.start()

    for p in range(3):
        settle(r1.at[p, pl.ds(0, 3)], 1, p)
        total = r1[p, 0].astype(F32) + r1[p, 1].astype(F32) + r1[p, 2].astype(F32) + r1[p, 3].astype(F32)
        S2[p] = total.astype(BF).reshape(16, 16, 128)

        def give2(o, p=p):
            k = index2[p] ^ o
            remote(S2.at[p, k], r2.at[p, index2[p]], w_s.at[2, p], w_r.at[2, p], peer2(p, k)).start()

        loop(1, 16, give2)
        r2[p, index2[p]] = S2[p, index2[p]]
    half_b1 = bb1.at[pl.ds(0, 3)]
    wait_b1 = remote(half_b1, half_b1, b_s.at[1], b_r.at[1], twin)
    wait_b1.wait_recv()
    bb2[index2[0]] = bb1[0] + bb1[1] + bb1[2] + bb1[3]

    def give_bias(o):
        remote(bb2.at[index2[0]], bb2.at[index2[0]], b_s.at[2], b_r.at[2], peer2(0, index2[0] ^ o)).start()

    loop(1, 16, give_bias)

    back = trecv.at[pl.ds(0, DEVICES - 1)]
    wait_t = remote(back, back, t_s, t_r, twin)
    wait_t.wait_recv()
    edge_sum = dot(one_t[...], trecv[...].reshape(SLOTS, WIDTH))
    gsend[...] = edge_sum[SMALL:].astype(BF).reshape(SUB, GIANT, WIDTH)

    def give_giants(o):
        remote(gsend.at[u ^ o], grecv.at[u], gg_s, gg_r, (g, u ^ o)).start()

    loop(1, SUB, give_giants)
    grecv[u] = gsend[u]
    smalls[...] = edge_sum[:SMALL].astype(BF)
    put_small = pltpu.make_async_copy(smalls, small_out, out_sem.at[1])
    put_small.start()

    for p in range(3):
        settle(r2.at[p, pl.ds(0, 15)], 2, p)
        G[core, p, axis1[p], index2[p]] = jnp.sum(r2[p].astype(F32), axis=0).astype(BF)

        def share2(o, p=p):
            piece = G.at[core, p, axis1[p], index2[p]]
            remote(piece, piece, w_s.at[3, p], w_r.at[3, p], peer2(p, index2[p] ^ o)).start()

        loop(1, 16, share2)

    for p in range(3):
        settle(r2.at[p, pl.ds(0, 15)], 3, p)
        for o in range(1, 4):
            piece = G.at[core, p, axis1[p]]
            remote(piece, piece, w_s.at[4, p], w_r.at[4, p], peer1(p, axis1[p] ^ o)).start()

    half_g = grecv.at[pl.ds(0, SUB - 1)]
    wait_g = remote(half_g, half_g, gg_s, gg_r, twin)
    wait_g.wait_recv()
    giants[...] = jnp.sum(grecv[...].astype(F32), axis=0).astype(BF)
    put_giant = pltpu.make_async_copy(giants, giant_out, out_sem.at[2])
    put_giant.start()

    half_b2 = bb2.at[pl.ds(0, 15)]
    wait_b2 = remote(half_b2, half_b2, b_s.at[2], b_r.at[2], twin)
    wait_b2.wait_recv()
    bias = jnp.sum(bb2[...], axis=0)
    for i in range(4):
        bfin[:, 128 * i : 128 * i + 128] = bias[i : i + 1]
    put_bias = pltpu.make_async_copy(bfin, bias_out, out_sem.at[3])
    put_bias.start()

    puts = [put_nodes, put_small, put_giant, put_bias]
    for p in range(3):
        settle(r1.at[p, pl.ds(0, 3)], 4, p)
        remote(G.at[core, p], G.at[core, p], w_s.at[5, p], w_r.at[5, p], twin).start()
        puts.append(pltpu.make_async_copy(G.at[core, p], w_out.at[core, p], out_sem.at[4 + p]))
        puts[-1].start()
    for p in range(3):
        settle(r0.at[p], 5, p)
        puts.append(pltpu.make_async_copy(G.at[1 - core, p], w_out.at[1 - core, p], out_sem.at[7 + p]))
        puts[-1].start()

    others.wait_send()
    rows_in.wait_send()
    terms_in.wait_send()
    sent = esend.at[pl.ds(0, DEVICES - 1)]
    remote(sent, sent, e_s, e_r.at[0], twin).wait_send()
    for one in (wait_t, wait_b1, wait_b2, wait_g, *waits):
        one.wait_send()
    for one in puts:
        one.wait()


def layer(node_feats, node_grad, small_edges, giant_edges, pair_node, pair_edge, send_count, w_in, b_in, w_out):
    V = pltpu.VMEM
    dma = pltpu.SemaphoreType.DMA
    any_spec = pl.BlockSpec(memory_space=pl.ANY)
    wide = (DEVICES, CAP, WIDTH)
    shape = jax.ShapeDtypeStruct
    return pl.pallas_call(
        layer_kernel,
        out_shape=(
            shape((NODES, WIDTH), BF),
            shape((SMALL, WIDTH), BF),
            shape((GIANT, WIDTH), BF),
            shape((2, 3, 4, 16, 16, 128), BF),
            shape((1, WIDTH), F32),
        ),
        in_specs=[any_spec] * 10,
        out_specs=(any_spec,) * 5,
        scratch_shapes=[
            V((NODES, WIDTH), BF), V((NODES, WIDTH), BF), V((2 * WIDTH, WIDTH), BF), V((WIDTH, WIDTH), BF),
            V((1, WIDTH), F32), V((8, 128), I32), V((1, SLOTS), I32), V((1, 128), I32),
            V((EDGES, WIDTH), BF), V((EDGES, SLOTS), BF), V((SUB, 8, 128), I32), V((8, SUB, 128), I32), V((GRP, SUB, 128), I32),
            V((SLOTS, 128), I32), V((1, SLOTS), I32),
            V(wide, BF), V(wide, BF), V(wide, BF), V(wide, BF),
            V((SLOTS, WIDTH), BF), V((SLOTS, WIDTH), BF), V((SLOTS, WIDTH), BF), V((SLOTS, WIDTH), BF),
            V((NODES, WIDTH), BF), V((SMALL, WIDTH), BF), V((GIANT, WIDTH), BF),
            V((3 * WIDTH, WIDTH), F32), V((1, WIDTH), F32),
            V((2, 3, 4, 256, 128), BF), V((3, 4, 256, 128), BF),
            V((3, 4, 256, 128), BF), V((3, 4, 256, 128), BF),
            V((3, 16, 16, 128), BF), V((3, 16, 16, 128), BF), V((2, 3, 4, 16, 16, 128), BF),
            V((2, 8, 128), F32), V((4, 8, 128), F32), V((16, 8, 128), F32), V((1, WIDTH), F32),
            V((SUB, GIANT, WIDTH), BF), V((SUB, GIANT, WIDTH), BF),
            dma((10,)), dma((10,)), dma, dma, dma, dma, dma, dma, dma, dma((CHUNKS,)), dma, dma,
            dma((6, 3)), dma((6, 3)), dma((3,)), dma((3,)), dma, dma,
        ],
        compiler_params=pltpu.CompilerParams(
            collective_id=1, has_side_effects=True, vmem_limit_bytes=56 << 20
        ),
        name="layer",
    )(node_feats, node_grad, small_edges, giant_edges, pair_node, pair_edge, send_count, w_in, b_in, w_out)


def finish_kernel(
    nodes_in, small_in, giant_in, w_in, bias_in,
    nodes_out, small_out, giant_out, gi_out, gb_out, go_out,
    nodes, small, giant, bias, parts, wide, in_sem, out_sem,
):
    through = (
        (nodes_in, nodes, nodes_out), (small_in, small, small_out), (giant_in, giant, giant_out), (bias_in, bias, gb_out),
    )
    loads = [pltpu.make_async_copy(w_in.at[:, p], parts.at[:, p], in_sem.at[p]) for p in range(3)]
    loads += [pltpu.make_async_copy(a, b, in_sem.at[3 + i]) for i, (a, b, _) in enumerate(through)]
    for one in loads:
        one.start()
    puts = []
    for p in range(3):
        loads[p].wait()
        for h in range(2):
            for i in range(4):
                top, left = 256 * (i >> 1), 256 * h + 128 * (i & 1)
                wide[p, top : top + 256, left : left + 128] = parts[h, p, i].reshape(256, 128).astype(F32)
        out = gi_out.at[pl.ds(WIDTH * p, WIDTH)] if p < 2 else go_out
        puts.append(pltpu.make_async_copy(wide.at[p], out, out_sem.at[p]))
        puts[-1].start()
    for i, (_, a, b) in enumerate(through):
        loads[3 + i].wait()
        puts.append(pltpu.make_async_copy(a, b, out_sem.at[3 + i]))
        puts[-1].start()
    for one in puts:
        one.wait()


def finish(*arrays):
    any_spec = pl.BlockSpec(memory_space=pl.ANY)
    shape = jax.ShapeDtypeStruct
    return pl.pallas_call(
        finish_kernel,
        out_shape=(
            shape((NODES, WIDTH), BF), shape((SMALL, WIDTH), BF), shape((GIANT, WIDTH), BF),
            shape((2 * WIDTH, WIDTH), F32), shape((1, WIDTH), F32), shape((WIDTH, WIDTH), F32),
        ),
        in_specs=[any_spec] * 5,
        out_specs=(any_spec,) * 6,
        scratch_shapes=[
            pltpu.VMEM((NODES, WIDTH), BF), pltpu.VMEM((SMALL, WIDTH), BF), pltpu.VMEM((GIANT, WIDTH), BF),
            pltpu.VMEM((1, WIDTH), F32), pltpu.VMEM((2, 3, 4, 16, 16, 128), BF), pltpu.VMEM((3, WIDTH, WIDTH), F32),
            pltpu.SemaphoreType.DMA((7,)), pltpu.SemaphoreType.DMA((7,)),
        ],
        compiler_params=pltpu.CompilerParams(vmem_limit_bytes=60 << 20),
        name="finish",
    )(*arrays)


def shards(
    node_feats, node_grad, small_edges, giant_edges, pair_node, pair_edge, send_count, w_in, b_in, w_out
):
    out = finish(*layer(
        node_feats, node_grad, small_edges, giant_edges, pair_node.reshape(8, 128),
        pair_edge.reshape(1, SLOTS), send_count, w_in, b_in.reshape(1, WIDTH), w_out,
    ))
    return (*out[:4], out[4].reshape(WIDTH), out[5])


def solution(mesh):
    both = ("grp", "sub")
    placed = (
        P(both, None), P(both, None), P(both, None), P(both, None), P(both), P(both), P(both, None), P(), P(), P(),
    )
    return jax.shard_map(
        shards,
        mesh=mesh,
        in_specs=placed,
        out_specs=(P(both, None), P(both, None), P(both, None), P(), P(), P()),
        check_vma=False,
    )
```

```python
import jax
import jax.numpy as jnp
from jax import lax
from jax.experimental import pallas as pl
from jax.experimental.pallas import tpu as pltpu
from jax.sharding import PartitionSpec as P

MESH = pl.DeviceIdType.MESH
BF = jnp.bfloat16
F32 = jnp.float32
I32 = jnp.int32
DEVICES = 128
SUB = 8
GRP = 16
CAP = 8
SLOTS = 1024
WIDTH = 512
NODES = 2048
SMALL = 256
GIANT = 16
EDGES = SMALL + GIANT * SUB
CHUNKS = 4
FAR = (10, 9, 11, 6, 14, 2, 8, 5, 7, 13, 15, 1, 3, 4, 12)
PER = DEVICES // CHUNKS
ROWS = PER * CAP


def device_of(x, y, z, core):
    return (y * 4 + (z & 1) * 2 + core, x * 2 + (z >> 1))


def mask_of(s):
    core, par, y, x, zh = (s >> 6) & 1, (s >> 5) & 1, (s >> 3) & 3, (s >> 1) & 3, s & 1
    zl = par ^ (x & 1) ^ (y & 1)
    return (y << 5) | (zl << 4) | (core << 3) | (x << 1) | zh


def place(j):
    return (j // SUB, lax.rem(j, SUB))


def dot(a, b, ca=1, cb=0):
    return lax.dot_general(
        a, b, (((ca,), (cb,)), ((), ())), preferred_element_type=F32
    )


def remote(src, dst, send, recv, to):
    return pltpu.make_async_remote_copy(
        src_ref=src, dst_ref=dst, send_sem=send, recv_sem=recv, device_id=to, device_id_type=MESH
    )


def loop(low, high, step):
    def body(i, carry):
        step(i)
        return carry

    lax.fori_loop(low, high, body, 0)


def layer_kernel(
    nf_in, ng_in, small_in, giant_in, pn_in, pe_in, sc_in, win_in, bin_in, wout_in,
    nodes, smalls, giants, wide, bfin,
    nf, ng, win, wout, b_in, pn, pe, sc,
    etab, one_t, ix1, ixt, ix2, colb, rowb,
    esend, erecv, tsend, trecv, nd_all, og_all, pg_all, nt,
    gw, gb, S, r0, S1, r1, S2, r2, G, bb0, bb1, bb2, gsend, grecv,
    in_sem, gi_s, gi_r, i1_s, i1_r, i2_s, i2_r, e_s, e_r, t_s, t_r,
    w_s, w_r, b_s, b_r, gg_s, gg_r,
):
    g, u = lax.axis_index("grp"), lax.axis_index("sub")
    me = g * SUB + u
    y, zl, core, x, zh = g >> 2, (g >> 1) & 1, g & 1, u >> 1, u & 1
    z = zh * 2 + zl
    par = zl ^ (x & 1) ^ (y & 1)
    pm = (core << 6) | (par << 5) | (y << 3) | (x << 1) | zh
    there = (x, y, z)
    axis1 = (x, y, z)
    index2 = (y * 4 + z, z * 4 + x, x * 4 + y)

    def peer1(p, k):
        c = list(there)
        c[p] = k
        return device_of(c[0], c[1], c[2], core)

    def peer2(p, k):
        c = list(there)
        c[(p + 1) % 3] = k >> 2
        c[(p + 2) % 3] = k & 3
        return device_of(c[0], c[1], c[2], core)

    mine = pl.ds(pl.multiple_of(SMALL + u * GIANT, GIANT), GIANT)
    loads = [
        pltpu.make_async_copy(a, b, in_sem.at[i])
        for i, (a, b) in enumerate(
            (
                (pn_in, pn), (sc_in, sc), (giant_in, etab.at[mine]), (pe_in, pe),
                (small_in, etab.at[pl.ds(0, SMALL)]), (nf_in, nf), (ng_in, ng),
                (win_in, win), (wout_in, wout), (bin_in, b_in),
            )
        )
    ]
    for load in loads:
        load.start()

    barrier = pltpu.get_barrier_semaphore()
    loop(1, SUB, lambda o: pl.semaphore_signal(
        barrier, inc=1, device_id=(g, u ^ o), device_id_type=MESH))
    loop(1, GRP, lambda o: pl.semaphore_signal(
        barrier, inc=1, device_id=(g ^ o, u), device_id_type=MESH))

    loads[0].wait()
    loads[1].wait()
    r_at = lax.broadcasted_iota(I32, (8, 128), 0)
    l_at = lax.broadcasted_iota(I32, (8, 128), 1)
    spread = jnp.where((l_at >> 4) == r_at, sc[...].astype(F32), 0.0).astype(BF)
    j_at = lax.broadcasted_iota(I32, (128, 128), 0)
    p_at = lax.broadcasted_iota(I32, (128, 128), 1)
    expand = jnp.where((j_at & 15) == (p_at >> 3), 1.0, 0.0).astype(BF)
    counts = dot(spread, expand).astype(I32)
    packed = jnp.where((l_at & 7) < counts, pn[...] & (NODES - 1), 4095)
    ix1[u] = packed
    loads[2].wait()

    bb0[core] = jnp.zeros((8, 128), F32)

    pl.semaphore_wait(barrier, SUB + GRP - 2)

    for o in (5, 4, 7, 3, 6, 2, 1):
        remote(etab.at[mine], etab.at[mine], gi_s, gi_r, (g, u ^ o)).start()
    for o in (5, 4, 7, 3, 6, 2, 1):
        remote(ix1.at[u], ix1.at[u], i1_s, i1_r, (g, u ^ o)).start()
    loads[3].wait()
    one_t[...] = jnp.where(
        lax.broadcasted_iota(I32, (EDGES, SLOTS), 0) == pe[...], 1.0, 0.0
    ).astype(BF)
    loads[4].wait()

    others = remote(ix1.at[pl.ds(0, SUB - 1)], ix1.at[pl.ds(0, SUB - 1)], i1_s, i1_r, (g, u ^ 1))
    others.wait_recv()

    for r in range(8):
        ixt[r] = jnp.concatenate([ix1[k, r : r + 1, :] for k in range(SUB)], axis=0)

    def step2(o):
        h = g ^ o
        remote(ixt.at[h >> 1], ix2.at[g], i2_s, i2_r, (h, u)).start()

    loop(1, GRP, step2)
    ix2[g] = ixt[g >> 1]

    span = pl.ds(SMALL, (SUB - 1) * GIANT)
    rows_in = remote(etab.at[span], etab.at[span], gi_s, gi_r, (g, u ^ 1))
    rows_in.wait_recv()
    esend[...] = dot(one_t[...], etab[...], 0, 0).astype(BF).reshape(DEVICES, CAP, WIDTH)

    def send_rows(s):
        j = me ^ mask_of(s)
        remote(esend.at[j], erecv.at[pm], e_s, e_r.at[s >> 5], place(j)).start()

    loop(1, DEVICES, send_rows)
    erecv[pm] = esend[me]

    half = ix2.at[pl.ds(0, GRP - 1)]
    terms_in = remote(half, half, i2_s, i2_r, (g ^ 1, u))
    terms_in.wait_recv()
    table = ix2[...].reshape(DEVICES, 128)
    high, low = (table >> 8).astype(F32).astype(BF), (table & 255).astype(F32).astype(BF)

    def source(q):
        qy, qx = (q >> 3) & 3, (q >> 1) & 3
        qz = ((q >> 5) & 1) ^ (qx & 1) ^ (qy & 1)
        return (qy << 5) | (qz << 4) | (((q >> 6) & 1) << 3) | (qx << 1) | (q & 1)

    first = (me & 15) * CAP
    s_col = lax.broadcasted_iota(I32, (SLOTS, 128), 0)
    d_col = lax.broadcasted_iota(I32, (SLOTS, 128), 1)
    pick = jnp.where(source(s_col >> 3) == d_col, 1.0, 0.0).astype(BF)
    values = dot(pick, high) * 256.0 + dot(pick, low)
    values = jnp.where(d_col == first + (s_col & 7), values, 0.0)
    col = jnp.sum(values, axis=1, keepdims=True).astype(I32)
    colb[...] = jnp.broadcast_to(col, (SLOTS, 128))
    values = dot(high, pick, 0, 1) * 256.0 + dot(low, pick, 0, 1)
    l_row = lax.broadcasted_iota(I32, (128, SLOTS), 0)
    s_row = lax.broadcasted_iota(I32, (128, SLOTS), 1)
    values = jnp.where(l_row == first + (s_row & 7), values, 0.0)
    rowb[...] = jnp.sum(values, axis=0, keepdims=True).astype(I32)

    for load in loads[5:]:
        load.wait()
    gw[...] = jnp.zeros_like(gw)
    gb[...] = jnp.zeros_like(gb)

    def chunk(c, last=False):
        b = (pm >> 5) ^ c
        rows = pl.ds(pl.multiple_of(b * ROWS, ROWS), ROWS)
        blocks = pl.ds(pl.multiple_of(b * PER, PER), PER)
        at = colb[rows]
        lanes = lax.broadcasted_iota(I32, (ROWS, 128), 1)
        hot = jnp.concatenate(
            [jnp.where(at == lanes + k * 128, 1.0, 0.0).astype(BF) for k in range(NODES // 128)],
            axis=1,
        )
        nd = dot(hot, nf[...]).astype(BF)
        og = dot(hot, ng[...]).astype(BF)
        nd_all[rows] = nd
        og_all[rows] = og
        preact = dot(nd, win[pl.ds(0, WIDTH)]) + b_in[...]
        hid_grad = dot(og, wout[...], 1, 1)

        if last:
            w = erecv.at[pl.ds(0, PER)]
            remote(w, w, e_s, e_r.at[c], (g, u ^ 1)).wait_recv()
        else:

            @pl.when(c == 0)
            def _():
                w = erecv.at[pl.ds(0, PER - 1)]
                remote(w, w, e_s, e_r.at[0], (g, u ^ 1)).wait_recv()

            @pl.when(c > 0)
            def _():
                w = erecv.at[pl.ds(0, PER)]
                remote(w, w, e_s, e_r.at[c], (g, u ^ 1)).wait_recv()

        er = erecv[blocks].reshape(ROWS, WIDTH)
        preact = preact + dot(er, win[pl.ds(WIDTH, WIDTH)])
        logistic = jax.nn.sigmoid(preact)
        hidden = (preact * logistic).astype(BF)
        pg = (hid_grad * logistic * (1.0 + preact * (1.0 - logistic))).astype(BF)
        pg_all[rows] = pg

        def weights(k, left, right):
            gw[pl.ds(k * WIDTH, WIDTH)] += dot(left, right, 0, 0)
            if last:
                reduce0(k)

        def terms():
            term = dot(pg, win[pl.ds(WIDTH, WIDTH)], 1, 1).astype(BF)
            tsend[blocks] = term.reshape(PER, CAP, WIDTH)

        if not last:
            terms()
            send_terms(c)
        weights(0, nd, pg)
        weights(1, er, pg)
        weights(2, hidden, og)
        gb[...] += jnp.sum(pg.astype(F32), axis=0, keepdims=True)
        if last:
            terms()

    def send_terms(c):
        def one(s):
            remote(tsend.at[pm ^ s], trecv.at[me], t_s, t_r, place(me ^ mask_of(s))).start()

        loop(c * PER + jnp.where(c == 0, 1, 0), (c + 1) * PER, one)

    twin = (g ^ 1, u)

    def reduce0(p):
        for h in range(2):
            for i in range(4):
                top, left = WIDTH * p + 256 * (i >> 1), 256 * h + 128 * (i & 1)
                S[h, p, i] = gw[top : top + 256, left : left + 128].astype(BF)
        remote(S.at[1 - core, p], r0.at[p], w_s.at[0, p], w_r.at[0, p], twin).start()

    loop(0, CHUNKS - 1, chunk)
    chunk(CHUNKS - 1, True)
    trecv[me] = tsend[pm]
    for i in range(4):
        bb0[core, i : i + 1, :] = gb[:, 128 * i : 128 * i + 128]
    bias0 = remote(bb0.at[core], bb0.at[core], b_s.at[0], b_r.at[0], twin)
    bias0.start()

    nt[...] = dot(pg_all[...], win[pl.ds(0, WIDTH)], 1, 1).astype(BF)

    def node_tile(t):
        rows = pl.ds(pl.multiple_of(t * 256, 256), 256)
        hot = jnp.where(
            lax.broadcasted_iota(I32, (256, SLOTS), 0) + t * 256 == rowb[...], 1.0, 0.0
        ).astype(BF)
        nodes[rows] = (ng[rows].astype(F32) + dot(hot, nt[...])).astype(BF)

    def settle(ref, stage, p):
        done = remote(ref, ref, w_s.at[stage, p], w_r.at[stage, p], twin)
        done.wait_recv()
        waits.append(done)

    waits = [bias0]
    send_terms(CHUNKS - 1)
    loop(0, 2, node_tile)
    for p in range(3):
        settle(r0.at[p], 0, p)
        for i in range(4):
            rows, half = pl.ds(WIDTH * p + 256 * (i >> 1), 256), pl.ds(pl.multiple_of(256 * core + 128 * (i & 1), 128), 128)
            S1[p, i] = (gw[rows, half] + r0[p, i].astype(F32)).astype(BF)
        for o in (2, 1, 3):
            k = axis1[p] ^ o
            remote(S1.at[p, k], r1.at[p, axis1[p]], w_s.at[1, p], w_r.at[1, p], peer1(p, k)).start()
        r1[p, axis1[p]] = S1[p, axis1[p]]
    bias0.wait_recv()
    bb1[x] = bb0[0] + bb0[1]
    for o in (2, 1, 3):
        remote(bb1.at[x], bb1.at[x], b_s.at[1], b_r.at[1], peer1(0, x ^ o)).start()

    loop(2, NODES // 256, node_tile)

    for p in range(3):
        settle(r1.at[p, pl.ds(0, 3)], 1, p)
        total = r1[p, 0].astype(F32) + r1[p, 1].astype(F32) + r1[p, 2].astype(F32) + r1[p, 3].astype(F32)
        S2[p] = total.astype(BF).reshape(16, 16, 128)

        def give2(o, p=p):
            k = index2[p] ^ o
            remote(S2.at[p, k], r2.at[p, index2[p]], w_s.at[2, p], w_r.at[2, p], peer2(p, k)).start()

        for o in FAR:
            give2(o)
        r2[p, index2[p]] = S2[p, index2[p]]
    half_b1 = bb1.at[pl.ds(0, 3)]
    wait_b1 = remote(half_b1, half_b1, b_s.at[1], b_r.at[1], twin)
    wait_b1.wait_recv()
    bb2[index2[0]] = bb1[0] + bb1[1] + bb1[2] + bb1[3]

    def give_bias(o):
        remote(bb2.at[index2[0]], bb2.at[index2[0]], b_s.at[2], b_r.at[2], peer2(0, index2[0] ^ o)).start()

    loop(1, 16, give_bias)

    for p in range(3):
        settle(r2.at[p, pl.ds(0, 15)], 2, p)
        G[core, p, axis1[p], index2[p]] = jnp.sum(r2[p].astype(F32), axis=0).astype(BF)

        def share2(o, p=p):
            piece = G.at[core, p, axis1[p], index2[p]]
            remote(piece, piece, w_s.at[3, p], w_r.at[3, p], peer2(p, index2[p] ^ o)).start()

        for o in FAR:
            share2(o)


    back = trecv.at[pl.ds(0, DEVICES - 1)]
    wait_t = remote(back, back, t_s, t_r, twin)
    wait_t.wait_recv()
    edge_sum = dot(one_t[...], trecv[...].reshape(SLOTS, WIDTH))
    gsend[...] = edge_sum[SMALL:].astype(BF).reshape(SUB, GIANT, WIDTH)

    def give_giants(o):
        remote(gsend.at[u ^ o], grecv.at[u], gg_s, gg_r, (g, u ^ o)).start()

    loop(1, SUB, give_giants)
    grecv[u] = gsend[u]
    smalls[...] = edge_sum[:SMALL].astype(BF)

    for p in range(3):
        settle(r2.at[p, pl.ds(0, 15)], 3, p)
        for o in (2, 1, 3):
            piece = G.at[core, p, axis1[p]]
            remote(piece, piece, w_s.at[4, p], w_r.at[4, p], peer1(p, axis1[p] ^ o)).start()

    half_g = grecv.at[pl.ds(0, SUB - 1)]
    wait_g = remote(half_g, half_g, gg_s, gg_r, twin)
    wait_g.wait_recv()
    giants[...] = jnp.sum(grecv[...].astype(F32), axis=0).astype(BF)

    half_b2 = bb2.at[pl.ds(0, 15)]
    wait_b2 = remote(half_b2, half_b2, b_s.at[2], b_r.at[2], twin)
    wait_b2.wait_recv()
    bias = jnp.sum(bb2[...], axis=0)
    for i in range(4):
        bfin[:, 128 * i : 128 * i + 128] = bias[i : i + 1]


    def widen(h, p):
        for i in range(4):
            top, left = 256 * (i >> 1), pl.multiple_of(256 * h + 128 * (i & 1), 128)
            wide[p, top : top + 256, pl.ds(left, 128)] = G[h, p, i].reshape(256, 128).astype(F32)

    for p in range(3):
        settle(r1.at[p, pl.ds(0, 3)], 4, p)
        remote(G.at[core, p], G.at[core, p], w_s.at[5, p], w_r.at[5, p], twin).start()
    for p in range(3):
        widen(core, p)
    for p in range(3):
        settle(r0.at[p], 5, p)
        widen(1 - core, p)

    others.wait_send()
    rows_in.wait_send()
    terms_in.wait_send()
    sent = esend.at[pl.ds(0, DEVICES - 1)]
    remote(sent, sent, e_s, e_r.at[0], twin).wait_send()
    for one in (wait_t, wait_b1, wait_b2, wait_g, *waits):
        one.wait_send()


def layer(*arrays):
    V = pltpu.VMEM
    dma = pltpu.SemaphoreType.DMA
    any_spec = pl.BlockSpec(memory_space=pl.ANY)
    wide = (DEVICES, CAP, WIDTH)
    return pl.pallas_call(
        layer_kernel,
        out_shape=(
            V((NODES, WIDTH), BF),
            V((SMALL, WIDTH), BF),
            V((GIANT, WIDTH), BF),
            V((3, WIDTH, WIDTH), F32),
            V((1, WIDTH), F32),
        ),
        in_specs=[any_spec] * 10,
        out_specs=(pl.BlockSpec(memory_space=V),) * 5,
        scratch_shapes=[
            V((NODES, WIDTH), BF), V((NODES, WIDTH), BF), V((2 * WIDTH, WIDTH), BF), V((WIDTH, WIDTH), BF),
            V((1, WIDTH), F32), V((8, 128), I32), V((1, SLOTS), I32), V((1, 128), I32),
            V((EDGES, WIDTH), BF), V((EDGES, SLOTS), BF), V((SUB, 8, 128), I32), V((8, SUB, 128), I32), V((GRP, SUB, 128), I32),
            V((SLOTS, 128), I32), V((1, SLOTS), I32),
            V(wide, BF), V(wide, BF), V(wide, BF), V(wide, BF),
            V((SLOTS, WIDTH), BF), V((SLOTS, WIDTH), BF), V((SLOTS, WIDTH), BF), V((SLOTS, WIDTH), BF),
            V((3 * WIDTH, WIDTH), F32), V((1, WIDTH), F32),
            V((2, 3, 4, 256, 128), BF), V((3, 4, 256, 128), BF),
            V((3, 4, 256, 128), BF), V((3, 4, 256, 128), BF),
            V((3, 16, 16, 128), BF), V((3, 16, 16, 128), BF), V((2, 3, 4, 16, 16, 128), BF),
            V((2, 8, 128), F32), V((4, 8, 128), F32), V((16, 8, 128), F32),
            V((SUB, GIANT, WIDTH), BF), V((SUB, GIANT, WIDTH), BF),
            dma((10,)), dma, dma, dma, dma, dma, dma, dma, dma((CHUNKS,)), dma, dma,
            dma((6, 3)), dma((6, 3)), dma((3,)), dma((3,)), dma, dma,
        ],
        compiler_params=pltpu.CompilerParams(
            collective_id=1, has_side_effects=True, vmem_limit_bytes=48 << 20
        ),
        name="layer",
    )(*[pltpu.with_memory_space_constraint(a, pltpu.HBM) for a in arrays])


def finish_kernel(nodes, small, giant, wide, bias, nodes_out, small_out, giant_out, gi_out, gb_out, go_out, sem):
    pairs = [(wide.at[p], gi_out.at[pl.ds(WIDTH * p, WIDTH)]) for p in range(2)] + [(wide.at[2], go_out)]
    pairs += [(nodes, nodes_out), (small, small_out), (giant, giant_out), (bias, gb_out)]
    puts = [pltpu.make_async_copy(a, b, sem.at[i]) for i, (a, b) in enumerate(pairs)]
    for one in puts:
        one.start()
    for one in puts:
        one.wait()


def finish(*arrays):
    held = [pltpu.with_memory_space_constraint(a, pltpu.VMEM) for a in arrays]
    shape = jax.ShapeDtypeStruct
    return pl.pallas_call(
        finish_kernel,
        out_shape=(
            shape((NODES, WIDTH), BF), shape((SMALL, WIDTH), BF), shape((GIANT, WIDTH), BF),
            shape((2 * WIDTH, WIDTH), F32), shape((1, WIDTH), F32), shape((WIDTH, WIDTH), F32),
        ),
        in_specs=[pl.BlockSpec(memory_space=pltpu.VMEM)] * 5,
        out_specs=(pl.BlockSpec(memory_space=pl.ANY),) * 6,
        scratch_shapes=[pltpu.SemaphoreType.DMA((7,))],
        compiler_params=pltpu.CompilerParams(vmem_limit_bytes=16 << 20),
        name="finish",
    )(*held)


def shards(
    node_feats, node_grad, small_edges, giant_edges, pair_node, pair_edge, send_count, w_in, b_in, w_out
):
    out = finish(*layer(
        node_feats, node_grad, small_edges, giant_edges, pair_node.reshape(8, 128),
        pair_edge.reshape(1, SLOTS), send_count, w_in, b_in.reshape(1, WIDTH), w_out,
    ))
    return (*out[:4], out[4].reshape(WIDTH), out[5])


def solution(mesh):
    both = ("grp", "sub")
    placed = (
        P(both, None), P(both, None), P(both, None), P(both, None), P(both), P(both), P(both, None), P(), P(), P(),
    )
    return jax.shard_map(
        shards,
        mesh=mesh,
        in_specs=placed,
        out_specs=(P(both, None), P(both, None), P(both, None), P(), P(), P()),
        check_vma=False,
    )
```

```python
import jax
import jax.numpy as jnp
from jax import lax
from jax.experimental import pallas as pl
from jax.experimental.pallas import tpu as pltpu
from jax.sharding import PartitionSpec as P

MESH = pl.DeviceIdType.MESH
BF = jnp.bfloat16
F32 = jnp.float32
I32 = jnp.int32
DEVICES = 128
SUB = 8
GRP = 16
CAP = 8
SLOTS = 1024
WIDTH = 512
NODES = 2048
SMALL = 256
GIANT = 16
EDGES = SMALL + GIANT * SUB
CHUNKS = 8
FAR = (10, 9, 11, 6, 14, 2, 8, 5, 7, 13, 15, 1, 3, 4, 12)
PER = DEVICES // CHUNKS
ROWS = PER * CAP


def device_of(x, y, z, core):
    return (y * 4 + (z & 1) * 2 + core, x * 2 + (z >> 1))


def mask_of(s):
    core, y, x = (s >> 6) & 1, (s >> 2) & 3, s & 3
    zl = ((s >> 5) & 1) ^ (x & 1) ^ (y & 1)
    zh = ((s >> 4) & 1) ^ (x >> 1) ^ (y >> 1)
    return (y << 5) | (zl << 4) | (core << 3) | (x << 1) | zh


def place(j):
    return (j // SUB, lax.rem(j, SUB))


def dot(a, b, ca=1, cb=0):
    return lax.dot_general(
        a, b, (((ca,), (cb,)), ((), ())), preferred_element_type=F32
    )


def remote(src, dst, send, recv, to):
    return pltpu.make_async_remote_copy(
        src_ref=src, dst_ref=dst, send_sem=send, recv_sem=recv, device_id=to, device_id_type=MESH
    )


def loop(low, high, step):
    def body(i, carry):
        step(i)
        return carry

    lax.fori_loop(low, high, body, 0)


def layer_kernel(
    nf_in, ng_in, small_in, giant_in, pn_in, pe_in, sc_in, win_in, bin_in, wout_in,
    nodes, smalls, giants, wide, bfin,
    nf, ng, win, wout, b_in, pn, pe, sc,
    etab, one_t, ix1, ixt, ix2, colb, rowb,
    esend, erecv, tsend, trecv, nd_all, og_all, pg_all, hid_all, nt, pre_n, hid_n,
    gw, gb, S, r0, S1, r1, S2, r2, G, bb0, bb1, bb2, gsend, grecv,
    in_sem, gi_s, gi_r, i1_s, i1_r, i2_s, i2_r, e_s, e_r, t_s, t_r,
    w_s, w_r, b_s, b_r, gg_s, gg_r,
):
    g, u = lax.axis_index("grp"), lax.axis_index("sub")
    me = g * SUB + u
    y, zl, core, x, zh = g >> 2, (g >> 1) & 1, g & 1, u >> 1, u & 1
    z = zh * 2 + zl
    pm = (core << 6) | ((zl ^ (x & 1) ^ (y & 1)) << 5) | ((zh ^ (x >> 1) ^ (y >> 1)) << 4) | (y << 2) | x
    there = (x, y, z)
    axis1 = (x, y, z)
    index2 = (y * 4 + z, z * 4 + x, x * 4 + y)

    def peer1(p, k):
        c = list(there)
        c[p] = k
        return device_of(c[0], c[1], c[2], core)

    def peer2(p, k):
        c = list(there)
        c[(p + 1) % 3] = k >> 2
        c[(p + 2) % 3] = k & 3
        return device_of(c[0], c[1], c[2], core)

    mine = pl.ds(pl.multiple_of(SMALL + u * GIANT, GIANT), GIANT)
    loads = [
        pltpu.make_async_copy(a, b, in_sem.at[i])
        for i, (a, b) in enumerate(
            (
                (pn_in, pn), (sc_in, sc), (giant_in, etab.at[mine]), (pe_in, pe),
                (small_in, etab.at[pl.ds(0, SMALL)]), (nf_in, nf), (ng_in, ng),
                (win_in, win), (wout_in, wout), (bin_in, b_in),
            )
        )
    ]
    for load in loads:
        load.start()

    barrier = pltpu.get_barrier_semaphore()
    loop(1, SUB, lambda o: pl.semaphore_signal(
        barrier, inc=1, device_id=(g, u ^ o), device_id_type=MESH))
    loop(1, GRP, lambda o: pl.semaphore_signal(
        barrier, inc=1, device_id=(g ^ o, u), device_id_type=MESH))

    loads[0].wait()
    loads[1].wait()
    r_at = lax.broadcasted_iota(I32, (8, 128), 0)
    l_at = lax.broadcasted_iota(I32, (8, 128), 1)
    spread = jnp.where((l_at >> 4) == r_at, sc[...].astype(F32), 0.0).astype(BF)
    j_at = lax.broadcasted_iota(I32, (128, 128), 0)
    p_at = lax.broadcasted_iota(I32, (128, 128), 1)
    expand = jnp.where((j_at & 15) == (p_at >> 3), 1.0, 0.0).astype(BF)
    counts = dot(spread, expand).astype(I32)
    packed = jnp.where((l_at & 7) < counts, pn[...] & (NODES - 1), 4095)
    ix1[u] = packed
    loads[2].wait()

    bb0[core] = jnp.zeros((8, 128), F32)

    pl.semaphore_wait(barrier, SUB + GRP - 2)

    for o in (5, 4, 7, 3, 6, 2, 1):
        remote(etab.at[mine], etab.at[mine], gi_s, gi_r, (g, u ^ o)).start()
    for o in (5, 4, 7, 3, 6, 2, 1):
        remote(ix1.at[u], ix1.at[u], i1_s, i1_r, (g, u ^ o)).start()
    loads[3].wait()
    one_t[...] = jnp.where(
        lax.broadcasted_iota(I32, (EDGES, SLOTS), 0) == pe[...], 1.0, 0.0
    ).astype(BF)
    loads[4].wait()

    span = pl.ds(SMALL, (SUB - 1) * GIANT)
    rows_in = remote(etab.at[span], etab.at[span], gi_s, gi_r, (g, u ^ 1))
    rows_in.wait_recv()
    esend[...] = dot(one_t[...], etab[...], 0, 0).astype(BF).reshape(DEVICES, CAP, WIDTH)

    others = remote(ix1.at[pl.ds(0, SUB - 1)], ix1.at[pl.ds(0, SUB - 1)], i1_s, i1_r, (g, u ^ 1))
    others.wait_recv()

    for r in range(8):
        ixt[r] = jnp.concatenate([ix1[k, r : r + 1, :] for k in range(SUB)], axis=0)

    def step2(o):
        h = g ^ o
        remote(ixt.at[h >> 1], ix2.at[g], i2_s, i2_r, (h, u)).start()

    loop(1, GRP, step2)
    ix2[g] = ixt[g >> 1]

    def each_peer(c, step):
        for i in range(1, PER):
            step(c * PER + i)

        if isinstance(c, int):
            step(c * PER)
        else:
            pl.when(c > 0)(lambda: step(c * PER))

    def send_rows(s):
        j = me ^ mask_of(s)
        remote(esend.at[j], erecv.at[pm], e_s, e_r.at[s // PER], place(j)).start()

    loop(0, CHUNKS, lambda c: each_peer(c, send_rows))
    erecv[pm] = esend[me]

    half = ix2.at[pl.ds(0, GRP - 1)]
    terms_in = remote(half, half, i2_s, i2_r, (g ^ 1, u))
    terms_in.wait_recv()
    table = ix2[...].reshape(DEVICES, 128)
    high, low = (table >> 8).astype(F32).astype(BF), (table & 255).astype(F32).astype(BF)

    first = (me & 15) * CAP
    s_col = lax.broadcasted_iota(I32, (SLOTS, 128), 0)
    d_col = lax.broadcasted_iota(I32, (SLOTS, 128), 1)
    pick = jnp.where(mask_of(s_col >> 3) == d_col, 1.0, 0.0).astype(BF)
    values = dot(pick, high) * 256.0 + dot(pick, low)
    values = jnp.where(d_col == first + (s_col & 7), values, 0.0)
    col = jnp.sum(values, axis=1, keepdims=True).astype(I32)
    colb[...] = jnp.broadcast_to(col, (SLOTS, 128))
    for load in loads[5:]:
        load.wait()
    gw[...] = jnp.zeros_like(gw)
    gb[...] = jnp.zeros_like(gb)

    def gather(k):
        rows = pl.ds(pl.multiple_of(k * 256, 256), 256)
        at = colb[rows]
        lanes = lax.broadcasted_iota(I32, (256, 128), 1)
        hot = jnp.concatenate(
            [jnp.where(at == lanes + k * 128, 1.0, 0.0).astype(BF) for k in range(NODES // 128)],
            axis=1,
        )
        nd = dot(hot, nf[...]).astype(BF)
        og = dot(hot, ng[...]).astype(BF)
        nd_all[rows] = nd
        og_all[rows] = og
        pre_n[rows] = dot(nd, win[pl.ds(0, WIDTH)]) + b_in[...]
        hid_n[rows] = dot(og, wout[...], 1, 1)

    gather(pm >> 5)

    def arrive(c):
        full = erecv.at[pl.ds(0, PER)]
        part = erecv.at[pl.ds(0, PER - 1)]
        if isinstance(c, int):
            remote(full, full, e_s, e_r.at[c], (g, u ^ 1)).wait_recv()
            return

        @pl.when(c == 0)
        def _():
            remote(part, part, e_s, e_r.at[0], (g, u ^ 1)).wait_recv()

        @pl.when(c > 0)
        def _():
            remote(full, full, e_s, e_r.at[c], (g, u ^ 1)).wait_recv()

    def chunk(c, last=False):
        b = (pm >> 4) ^ c
        rows = pl.ds(pl.multiple_of(b * ROWS, ROWS), ROWS)
        blocks = pl.ds(pl.multiple_of(b * PER, PER), PER)
        arrive(c)
        er = erecv[blocks].reshape(ROWS, WIDTH)
        preact = pre_n[rows] + dot(er, win[pl.ds(WIDTH, WIDTH)])
        logistic = jax.nn.sigmoid(preact)
        hid_all[rows] = (preact * logistic).astype(BF)
        pg = (hid_n[rows] * logistic * (1.0 + preact * (1.0 - logistic))).astype(BF)
        pg_all[rows] = pg
        gb[...] += jnp.sum(pg.astype(F32), axis=0, keepdims=True)
        if not last:
            terms(b)
            send_terms(c)

    def terms(b):
        rows = pl.ds(pl.multiple_of(b * ROWS, ROWS), ROWS)
        term = dot(pg_all[rows], win[pl.ds(WIDTH, WIDTH)], 1, 1).astype(BF)
        tsend[pl.ds(pl.multiple_of(b * PER, PER), PER)] = term.reshape(PER, CAP, WIDTH)

    def weights(k, last=False):
        b = (pm >> 5) ^ k
        rows = pl.ds(pl.multiple_of(b * 256, 256), 256)
        er = erecv[pl.ds(pl.multiple_of(b * 32, 32), 32)].reshape(256, WIDTH)
        for p, (left, right) in enumerate(((nd_all[rows], pg_all[rows]), (er, pg_all[rows]), (hid_all[rows], og_all[rows]))):
            gw[pl.ds(p * WIDTH, WIDTH)] += dot(left, right, 0, 0)
            if last:
                reduce0(p)

    def send_terms(c):
        each_peer(c, lambda s: remote(tsend.at[pm ^ s], trecv.at[me], t_s, t_r, place(me ^ mask_of(s))).start())

    twin = (g ^ 1, u)

    def reduce0(p):
        for h in range(2):
            for i in range(4):
                top, left = WIDTH * p + 256 * (i >> 1), 256 * h + 128 * (i & 1)
                S[h, p, i] = gw[top : top + 256, left : left + 128].astype(BF)
        remote(S.at[1 - core, p], r0.at[p], w_s.at[0, p], w_r.at[0, p], twin).start()

    def pair(k):
        chunk(2 * k)
        chunk(2 * k + 1)
        gather((pm >> 5) ^ (k + 1))
        weights(k)

    loop(0, CHUNKS // 2 - 1, pair)
    chunk(CHUNKS - 2)
    chunk(CHUNKS - 1, True)
    terms((pm >> 4) ^ (CHUNKS - 1))
    send_terms(CHUNKS - 1)
    weights(CHUNKS // 2 - 1, True)
    trecv[me] = tsend[pm]
    for i in range(4):
        bb0[core, i : i + 1, :] = gb[:, 128 * i : 128 * i + 128]
    bias0 = remote(bb0.at[core], bb0.at[core], b_s.at[0], b_r.at[0], twin)
    bias0.start()

    values = dot(high, pick, 0, 1) * 256.0 + dot(low, pick, 0, 1)
    l_row = lax.broadcasted_iota(I32, (128, SLOTS), 0)
    s_row = lax.broadcasted_iota(I32, (128, SLOTS), 1)
    values = jnp.where(l_row == first + (s_row & 7), values, 0.0)
    rowb[...] = jnp.sum(values, axis=0, keepdims=True).astype(I32)

    nt[...] = dot(pg_all[...], win[pl.ds(0, WIDTH)], 1, 1).astype(BF)

    def node_tile(t):
        rows = pl.ds(pl.multiple_of(t * 256, 256), 256)
        hot = jnp.where(
            lax.broadcasted_iota(I32, (256, SLOTS), 0) + t * 256 == rowb[...], 1.0, 0.0
        ).astype(BF)
        nodes[rows] = (ng[rows].astype(F32) + dot(hot, nt[...])).astype(BF)

    def settle(ref, stage, p):
        done = remote(ref, ref, w_s.at[stage, p], w_r.at[stage, p], twin)
        done.wait_recv()
        waits.append(done)

    waits = [bias0]
    loop(0, 2, node_tile)
    for p in range(3):
        settle(r0.at[p], 0, p)
        for i in range(4):
            rows, half = pl.ds(WIDTH * p + 256 * (i >> 1), 256), pl.ds(pl.multiple_of(256 * core + 128 * (i & 1), 128), 128)
            S1[p, i] = (gw[rows, half] + r0[p, i].astype(F32)).astype(BF)
        for o in (2, 1, 3):
            k = axis1[p] ^ o
            remote(S1.at[p, k], r1.at[p, axis1[p]], w_s.at[1, p], w_r.at[1, p], peer1(p, k)).start()
        r1[p, axis1[p]] = S1[p, axis1[p]]
    bias0.wait_recv()
    bb1[x] = bb0[0] + bb0[1]
    for o in (2, 1, 3):
        remote(bb1.at[x], bb1.at[x], b_s.at[1], b_r.at[1], peer1(0, x ^ o)).start()

    loop(2, NODES // 256, node_tile)

    for p in range(3):
        settle(r1.at[p, pl.ds(0, 3)], 1, p)
        total = r1[p, 0].astype(F32) + r1[p, 1].astype(F32) + r1[p, 2].astype(F32) + r1[p, 3].astype(F32)
        S2[p] = total.astype(BF).reshape(16, 16, 128)

        def give2(o, p=p):
            k = index2[p] ^ o
            remote(S2.at[p, k], r2.at[p, index2[p]], w_s.at[2, p], w_r.at[2, p], peer2(p, k)).start()

        for o in FAR:
            give2(o)
        r2[p, index2[p]] = S2[p, index2[p]]
    half_b1 = bb1.at[pl.ds(0, 3)]
    wait_b1 = remote(half_b1, half_b1, b_s.at[1], b_r.at[1], twin)
    wait_b1.wait_recv()
    bb2[index2[0]] = bb1[0] + bb1[1] + bb1[2] + bb1[3]

    def give_bias(o):
        remote(bb2.at[index2[0]], bb2.at[index2[0]], b_s.at[2], b_r.at[2], peer2(0, index2[0] ^ o)).start()

    loop(1, 16, give_bias)

    for p in range(3):
        settle(r2.at[p, pl.ds(0, 15)], 2, p)
        G[core, p, axis1[p], index2[p]] = jnp.sum(r2[p].astype(F32), axis=0).astype(BF)

        def share2(o, p=p):
            piece = G.at[core, p, axis1[p], index2[p]]
            remote(piece, piece, w_s.at[3, p], w_r.at[3, p], peer2(p, index2[p] ^ o)).start()

        for o in FAR:
            share2(o)


    back = trecv.at[pl.ds(0, DEVICES - 1)]
    wait_t = remote(back, back, t_s, t_r, twin)
    wait_t.wait_recv()
    edge_sum = dot(one_t[...], trecv[...].reshape(SLOTS, WIDTH))
    gsend[...] = edge_sum[SMALL:].astype(BF).reshape(SUB, GIANT, WIDTH)

    def give_giants(o):
        remote(gsend.at[u ^ o], grecv.at[u], gg_s, gg_r, (g, u ^ o)).start()

    loop(1, SUB, give_giants)
    grecv[u] = gsend[u]
    smalls[...] = edge_sum[:SMALL].astype(BF)

    for p in range(3):
        settle(r2.at[p, pl.ds(0, 15)], 3, p)
        for o in (2, 1, 3):
            piece = G.at[core, p, axis1[p]]
            remote(piece, piece, w_s.at[4, p], w_r.at[4, p], peer1(p, axis1[p] ^ o)).start()

    half_g = grecv.at[pl.ds(0, SUB - 1)]
    wait_g = remote(half_g, half_g, gg_s, gg_r, twin)
    wait_g.wait_recv()
    giants[...] = jnp.sum(grecv[...].astype(F32), axis=0).astype(BF)

    half_b2 = bb2.at[pl.ds(0, 15)]
    wait_b2 = remote(half_b2, half_b2, b_s.at[2], b_r.at[2], twin)
    wait_b2.wait_recv()
    bias = jnp.sum(bb2[...], axis=0)
    for i in range(4):
        bfin[:, 128 * i : 128 * i + 128] = bias[i : i + 1]


    def widen(h, p):
        for i in range(4):
            top, left = 256 * (i >> 1), pl.multiple_of(256 * h + 128 * (i & 1), 128)
            wide[p, top : top + 256, pl.ds(left, 128)] = G[h, p, i].reshape(256, 128).astype(F32)

    for p in range(3):
        settle(r1.at[p, pl.ds(0, 3)], 4, p)
        remote(G.at[core, p], G.at[core, p], w_s.at[5, p], w_r.at[5, p], twin).start()
    for p in range(3):
        widen(core, p)
    for p in range(3):
        settle(r0.at[p], 5, p)
        widen(1 - core, p)

    others.wait_send()
    rows_in.wait_send()
    terms_in.wait_send()
    sent = esend.at[pl.ds(0, DEVICES - 1)]
    remote(sent, sent, e_s, e_r.at[0], twin).wait_send()
    for one in (wait_t, wait_b1, wait_b2, wait_g, *waits):
        one.wait_send()


def layer(*arrays):
    V = pltpu.VMEM
    dma = pltpu.SemaphoreType.DMA
    any_spec = pl.BlockSpec(memory_space=pl.ANY)
    wide = (DEVICES, CAP, WIDTH)
    return pl.pallas_call(
        layer_kernel,
        out_shape=(
            V((NODES, WIDTH), BF),
            V((SMALL, WIDTH), BF),
            V((GIANT, WIDTH), BF),
            V((3, WIDTH, WIDTH), F32),
            V((1, WIDTH), F32),
        ),
        in_specs=[any_spec] * 10,
        out_specs=(pl.BlockSpec(memory_space=V),) * 5,
        scratch_shapes=[
            V((NODES, WIDTH), BF), V((NODES, WIDTH), BF), V((2 * WIDTH, WIDTH), BF), V((WIDTH, WIDTH), BF),
            V((1, WIDTH), F32), V((8, 128), I32), V((1, SLOTS), I32), V((1, 128), I32),
            V((EDGES, WIDTH), BF), V((EDGES, SLOTS), BF), V((SUB, 8, 128), I32), V((8, SUB, 128), I32), V((GRP, SUB, 128), I32),
            V((SLOTS, 128), I32), V((1, SLOTS), I32),
            V(wide, BF), V(wide, BF), V(wide, BF), V(wide, BF),
            V((SLOTS, WIDTH), BF), V((SLOTS, WIDTH), BF), V((SLOTS, WIDTH), BF), V((SLOTS, WIDTH), BF),
            V((SLOTS, WIDTH), BF), V((SLOTS, WIDTH), F32), V((SLOTS, WIDTH), F32),
            V((3 * WIDTH, WIDTH), F32), V((1, WIDTH), F32),
            V((2, 3, 4, 256, 128), BF), V((3, 4, 256, 128), BF),
            V((3, 4, 256, 128), BF), V((3, 4, 256, 128), BF),
            V((3, 16, 16, 128), BF), V((3, 16, 16, 128), BF), V((2, 3, 4, 16, 16, 128), BF),
            V((2, 8, 128), F32), V((4, 8, 128), F32), V((16, 8, 128), F32),
            V((SUB, GIANT, WIDTH), BF), V((SUB, GIANT, WIDTH), BF),
            dma((10,)), dma, dma, dma, dma, dma, dma, dma, dma((CHUNKS,)), dma, dma,
            dma((6, 3)), dma((6, 3)), dma((3,)), dma((3,)), dma, dma,
        ],
        compiler_params=pltpu.CompilerParams(
            collective_id=1, has_side_effects=True, vmem_limit_bytes=48 << 20
        ),
        name="layer",
    )(*[pltpu.with_memory_space_constraint(a, pltpu.HBM) for a in arrays])


def finish_kernel(nodes, small, giant, wide, bias, nodes_out, small_out, giant_out, gi_out, gb_out, go_out, sem):
    pairs = [(wide.at[p], gi_out.at[pl.ds(WIDTH * p, WIDTH)]) for p in range(2)] + [(wide.at[2], go_out)]
    pairs += [(nodes, nodes_out), (small, small_out), (giant, giant_out), (bias, gb_out)]
    puts = [pltpu.make_async_copy(a, b, sem.at[i]) for i, (a, b) in enumerate(pairs)]
    for one in puts:
        one.start()
    for one in puts:
        one.wait()


def finish(*arrays):
    held = [pltpu.with_memory_space_constraint(a, pltpu.VMEM) for a in arrays]
    shape = jax.ShapeDtypeStruct
    return pl.pallas_call(
        finish_kernel,
        out_shape=(
            shape((NODES, WIDTH), BF), shape((SMALL, WIDTH), BF), shape((GIANT, WIDTH), BF),
            shape((2 * WIDTH, WIDTH), F32), shape((1, WIDTH), F32), shape((WIDTH, WIDTH), F32),
        ),
        in_specs=[pl.BlockSpec(memory_space=pltpu.VMEM)] * 5,
        out_specs=(pl.BlockSpec(memory_space=pl.ANY),) * 6,
        scratch_shapes=[pltpu.SemaphoreType.DMA((7,))],
        compiler_params=pltpu.CompilerParams(vmem_limit_bytes=16 << 20),
        name="finish",
    )(*held)


def shards(
    node_feats, node_grad, small_edges, giant_edges, pair_node, pair_edge, send_count, w_in, b_in, w_out
):
    out = finish(*layer(
        node_feats, node_grad, small_edges, giant_edges, pair_node.reshape(8, 128),
        pair_edge.reshape(1, SLOTS), send_count, w_in, b_in.reshape(1, WIDTH), w_out,
    ))
    return (*out[:4], out[4].reshape(WIDTH), out[5])


def solution(mesh):
    both = ("grp", "sub")
    placed = (
        P(both, None), P(both, None), P(both, None), P(both, None), P(both), P(both), P(both, None), P(), P(), P(),
    )
    return jax.shard_map(
        shards,
        mesh=mesh,
        in_specs=placed,
        out_specs=(P(both, None), P(both, None), P(both, None), P(), P(), P()),
        check_vma=False,
    )
```
